32 devices in a mesh: row: 8 (over z, y), col: 4 (over x, core).
Axes of the slice: x: 2, y: 2, z: 4, core: 2. Of those that a mesh axis runs over, the one named last changes fastest.
Arguments:
- density_values: float32 [2048, 512], P('row', 'col'), may hold values from -5 to 5
- density_cols: int32 [32, 8], P('row', 'col'), may hold values from 0 to 31, as said below
- ks_cols: int32 [32, 16], P('row', 'col'), may hold values from 0 to 31, as said below
- core_hamiltonian: float32 [2048, 1024], P('row', 'col'), may hold values from -3 to 3
- tile_blocks: int32 [64, 16], P('row'), may hold values from 0 to 31, as said below
- grid_weights: float32 [64, 128], P('row'), may hold values from 0.5 to 2
- basis_values: float32 [64, 128, 1024], P('row'), may hold values from -1.5 to 1.5
Outputs:
- kohn_sham: float32 [2048, 1024], P('row', 'col')
- purified: float32 [2048, 512], P('row', 'col')
The draws below stay inside these ranges and needn't reach their ends.
Inputs may be any that keep to these rules, and one draw needn't show every extreme that they name: `density_cols`: for each block row and each index c of col, the 2 entries in slots c * 2 .. c * 2 + 1 are different block columns of c * 8 .. c * 8 + 7. `ks_cols`: for each block row and each index c of col, the 4 entries in slots c * 4 .. c * 4 + 3 are different block columns of c * 8 .. c * 8 + 7. `tile_blocks`: each tile names 16 different blocks.
All inputs are finite; a program needn't handle non-finite values.
Results may differ from the reference program's by a relative error of at most 0.0003.
Values sent between devices are 32-bit elements; how exact they have to be, the bound alone decides.
A program may use at most 128 MiB of HBM per device.

```python
import math
import jax
import jax.numpy as jnp
from jax import lax

BS = 64
TB = 16
G = 128
NZR = 2
NZK = 4
NB = 32
BC_DEV = 8
N = 2048
SLOTS = 8
KSLOTS = 16
TILES = 64
N_COL = 4


def chosen_offsets(key, rows, span, keep):
    scores = jax.random.randint(key, (rows, span), 0, 1048576)
    distinct = scores * span + jnp.arange(span, dtype=jnp.int32)[None, :]
    ordering = jnp.argsort(distinct, axis=1)
    ranking = jnp.argsort(ordering, axis=1)
    chosen = (ranking < keep).astype(jnp.int32)
    slots = jnp.cumsum(chosen, axis=1) - 1
    picked = (chosen[:, None, :] == 1) & (slots[:, None, :] == jnp.arange(keep, dtype=jnp.int32)[None, :, None])
    return jnp.sum(jnp.where(picked, jnp.arange(span, dtype=jnp.int32)[None, None, :], 0), axis=2).astype(jnp.int32)


def band_columns(key, keep):
    groups = NB // BC_DEV
    span = 2 * keep
    offsets = chosen_offsets(key, NB * groups, span, keep).reshape(NB, groups, keep) - keep
    centre = jnp.arange(NB, dtype=jnp.int32) % BC_DEV
    local_ids = (centre[:, None, None] + offsets + BC_DEV) % BC_DEV
    columns = jnp.arange(groups, dtype=jnp.int32)[None, :, None] * BC_DEV + local_ids
    return columns.reshape(NB, groups * keep).astype(jnp.int32)


def draw_density_cols(key, part):
    return band_columns(jax.random.fold_in(key, 11), NZR)


def draw_ks_cols(key, part):
    return band_columns(jax.random.fold_in(key, 23), NZK)


def draw_tile_blocks(key, part):
    key_start, key_pick = jax.random.split(jax.random.fold_in(key, 41), 2)
    groups = NB // BC_DEV
    starts = jax.random.randint(key_start, (TILES,), 0, NB)
    offsets = chosen_offsets(key_pick, TILES, 2 * TB, TB)
    spatial = (starts[:, None] + offsets) % NB
    return (spatial % groups * BC_DEV + spatial // groups).astype(jnp.int32)


def draw_density_values(key, part):
    key_entries, key_rows, key_cols = jax.random.split(jax.random.fold_in(key, 37), 3)
    width = NB // BC_DEV * NZR * BS
    row_place = jnp.arange(N, dtype=jnp.float32) / N
    trend = jnp.exp(row_place * math.log(3.0))
    entries = jnp.clip(jax.random.normal(key_entries, (N, width), jnp.float32), -4.0, 4.0)
    row_scale = trend * jnp.exp(math.log(10.0) * jax.random.uniform(key_rows, (N,), jnp.float32))
    col_scale = jnp.exp(math.log(4.0) * jax.random.uniform(key_cols, (width,), jnp.float32))
    return 0.01 * entries * row_scale[:, None] * col_scale[None, :]


def level_of(rng, shape, shards, smallest, largest):
    def one(axis_at, shards_of):
        steps = jax.random.uniform(jax.random.fold_in(jax.random.fold_in(rng, 6), axis_at), (shards_of,), jnp.float32, smallest / len(shards), largest / len(shards))
        return jnp.repeat(jnp.exp(steps), shape[axis_at] // shards_of).reshape((-1,) + (1,) * (len(shape) - axis_at - 1))

    level = one(*shards[0])
    for cut in shards[1:]:
        level = level * one(*cut)
    return level


def bell_draw(own_key, shape, deviation, limit, cuts=(), kind=jnp.bfloat16):
    array = jax.random.normal(own_key, shape, jnp.float32) * deviation
    if len(cuts) > 0:
        array = level_of(own_key, shape, cuts, -0.22, 0.18) * array
    return jnp.clip(array, min=-limit, max=limit).astype(kind)


def setup_inputs(seed: int = 0) -> dict:
    seeds = jax.random.split(jax.random.key(seed), 8)
    return {
        "density_values": draw_density_values(jax.random.fold_in(seeds[7], 71), 0),
        "density_cols": draw_density_cols(jax.random.fold_in(seeds[7], 71), 0),
        "ks_cols": draw_ks_cols(jax.random.fold_in(seeds[7], 71), 0),
        "core_hamiltonian": bell_draw(seeds[3], (N, KSLOTS * BS), 0.5, 3.0, ((0, 8), (1, 4)), jnp.float32),
        "tile_blocks": draw_tile_blocks(jax.random.fold_in(seeds[7], 71), 0),
        "grid_weights": jnp.clip(jnp.exp(math.log(2.0) - 1.3862944 * jax.random.uniform(seeds[5], (TILES, G), jnp.float32) ** level_of(seeds[5], (TILES, G), ((0, 8),), -0.2, 0.2)), 0.5, 2.0),
        "basis_values": bell_draw(seeds[6], (TILES, G, TB * BS), 0.25, 1.5, ((0, 8),), jnp.float32),
    }


def reference(density_values, density_cols, ks_cols, core_hamiltonian, tile_blocks, grid_weights, basis_values):
    highest = lax.Precision.HIGHEST
    dense_blocks = density_values.reshape(NB, BS, SLOTS, BS)

    def product_row(item):
        rows_here, cols_here = item
        neighbours = dense_blocks[cols_here].reshape(SLOTS, BS, N_COL, NZR, BS)
        their_cols = density_cols[cols_here].reshape(SLOTS, N_COL, NZR)
        matches = (their_cols[:, :, :, None] == cols_here.reshape(N_COL, NZR)[None, :, None, :]).astype(jnp.float32)
        combined = jnp.einsum('pcqr,pacqh->pcrah', matches, neighbours, precision=highest)
        return jnp.einsum('fpa,pcrah->fcrh', rows_here, combined, precision=highest).reshape(BS, SLOTS * BS)
    kept = lax.map(product_row, (dense_blocks, density_cols)).reshape(N, SLOTS * BS)
    mean_square = jnp.sum(kept * kept) / (N * SLOTS * BS)
    purified = kept / jnp.sqrt(mean_square + 1e-06)
    basis = basis_values.reshape(TILES, G, TB, BS)

    def tile_density(item):
        tile_ids, tile_basis = item
        rows_here = dense_blocks[tile_ids]
        cols_here = density_cols[tile_ids]
        halves = jnp.einsum('gif,ifsh->gish', tile_basis, rows_here, precision=highest)
        matches = (cols_here[:, :, None] == tile_ids[None, None, :]).astype(jnp.float32)
        combined = jnp.einsum('isj,gish->gjh', matches, halves, precision=highest)
        return lax.optimization_barrier(jnp.sum(combined * tile_basis, axis=(1, 2)))
    grid_density = lax.map(tile_density, (tile_blocks, basis))
    potential = grid_weights * jnp.tanh(grid_density)

    def add_tile(accumulated, item):
        tile_ids, tile_basis, tile_potential = item
        kept_cols = ks_cols[tile_ids]
        matches = (kept_cols[:, :, None] == tile_ids[None, None, :]).astype(jnp.float32)
        selected = jnp.einsum('isj,gjh->gish', matches, tile_basis, precision=highest)
        weighted = tile_basis * tile_potential[:, None, None]
        pairs = jnp.einsum('gif,gish->ifsh', weighted, selected, precision=highest)
        return (accumulated.at[tile_ids].add(pairs), None)
    start_sum = jnp.zeros((NB, BS, KSLOTS, BS), jnp.float32)
    accumulated, unused = lax.scan(add_tile, start_sum, (tile_blocks, basis, potential))
    kohn_sham = core_hamiltonian + accumulated.reshape(N, KSLOTS * BS)
    return (kohn_sham, purified)
```

```python
import functools
import jax
import jax.numpy as jnp
from jax import lax
from jax.experimental import pallas as pl
from jax.experimental.pallas import tpu as pltpu
from jax.sharding import PartitionSpec as P

BS = 64
TB = 16
G = 128
PAIR = 2 * BS
VMEM_BUDGET = 52 * 1024 * 1024


def split(x):
    high = x.astype(jnp.bfloat16)
    return high, (x - high.astype(jnp.float32)).astype(jnp.bfloat16)


def dot(a, b):
    return jnp.dot(a, b, preferred_element_type=jnp.float32)


def dot3(ah, al, bh, bl):
    return dot(ah, bh) + (dot(ah, bl) + dot(al, bh))


def lane_half():
    return (lax.broadcasted_iota(jnp.int32, (1, PAIR), 1) >= BS).astype(jnp.float32)


def widen(values, codes, out_h, out_l, row, first_lane, pairs):
    half = lane_half()
    swapped = pltpu.roll(values, BS, 1)
    swapped_codes = pltpu.roll(jnp.broadcast_to(codes, (8, PAIR)), BS, 1)[0:1]
    for p in range(pairs):
        block = 2.0 * p + half
        dense = jnp.where(codes == block, values, 0.0) + jnp.where(
            swapped_codes == block, swapped, 0.0
        )
        high, low = split(dense)
        lanes = pl.ds(first_lane + p * PAIR, PAIR)
        out_h[pl.ds(row, BS), lanes] = high
        out_l[pl.ds(row, BS), lanes] = low


def expand_kernel(places, basis, bh, bl, sources):
    tiles = basis.shape[0]
    source_pairs = basis.shape[2] // PAIR
    half = lane_half()
    sources[0, source_pairs] = jnp.zeros((G, PAIR), jnp.float32)
    sources[1, source_pairs] = jnp.zeros((G, PAIR), jnp.float32)

    @pl.loop(0, tiles)
    def _(t):
        for p in range(source_pairs):
            x = basis[t, :, p * PAIR : (p + 1) * PAIR]
            sources[0, p] = x
            sources[1, p] = pltpu.roll(x, BS, 1)
        rows = pl.ds(pl.multiple_of(t * G, G), G)
        for d in range(bh.shape[1] // PAIR):
            left = places[t, 2 * d]
            right = places[t, 2 * d + 1]
            dense = jnp.where(
                half == 0.0,
                sources[left % 2, left // 2],
                sources[1 - right % 2, right // 2],
            )
            high, low = split(dense)
            bh[rows, d * PAIR : (d + 1) * PAIR] = high
            bl[rows, d * PAIR : (d + 1) * PAIR] = low


def density_kernel(col, bh, bl, panel, codes, own, own_codes, my_codes, parts, kept, dh, dl, oh, ol):
    all_blocks = codes.shape[0]
    width = dh.shape[1]
    pairs = width // PAIR
    cols = own.shape[0]
    row_blocks = own_codes.shape[1]

    @pl.loop(0, all_blocks)
    def _(l):
        at = pl.multiple_of(l * BS, BS)
        widen(panel[pl.ds(at, BS), :], codes[pl.ds(l, 1), :], dh, dl, at, 0, pairs)

    for c in range(cols):
        for l in range(row_blocks):
            widen(
                own[c, l * BS : (l + 1) * BS, :],
                own_codes[c, l : l + 1, :],
                oh,
                ol,
                l * BS,
                c * width,
                pairs,
            )
    points = bh.shape[0]
    step = 4 * G
    first = pl.multiple_of(col[0] * width, PAIR)
    mine = pl.ds(first, width)

    @pl.loop(0, points // step)
    def _(s):
        rows = pl.ds(pl.multiple_of(s * step, step), step)
        x = dot3(bh[rows, :], bl[rows, :], dh[...], dl[...])
        local = bh[rows, mine].astype(jnp.float32) + bl[rows, mine].astype(jnp.float32)
        sums = jnp.sum(x * local, axis=1, keepdims=True)
        for t in range(step // G):
            tile = jnp.broadcast_to(sums[t * G : (t + 1) * G], (G, G))
            parts[pl.ds(s * (step // G) + t, 1), :] = tile.T[0:1, :]

    product = dot3(oh[...], ol[...], dh[...], dl[...])
    half = lane_half()
    total = jnp.zeros((BS, PAIR), jnp.float32)
    for l in range(row_blocks):
        codes_here = my_codes[l : l + 1, :]
        block = jnp.zeros((BS, PAIR), jnp.float32)
        for p in range(pairs):
            chunk = product[l * BS : (l + 1) * BS, p * PAIR : (p + 1) * PAIR]
            block += jnp.where(codes_here == 2.0 * p + half, chunk, 0.0)
            block += jnp.where(
                codes_here == 2.0 * p + 1.0 - half, pltpu.roll(chunk, BS, 1), 0.0
            )
        kept[l * BS : (l + 1) * BS, :] = block
        total += block * block
    square = jnp.sum(jnp.sum(total, axis=1, keepdims=True), axis=0, keepdims=True)
    tiles = points // G
    parts[tiles : tiles + 8, :] = jnp.broadcast_to(square, (8, PAIR))


def exchange_kernel(col, ks, bh, bl, sums, weights, out, wh, wl, chunk):
    points = bh.shape[0]
    tiles = points // G
    width = chunk.shape[0]
    row_count, out_rows, lanes = out.shape
    ks_slots = ks.shape[1]
    mine = pl.ds(pl.multiple_of(col[0] * width, PAIR), width)
    potential = weights[...] * jnp.tanh(sums[0:tiles, :])
    for t in range(tiles):
        rows = pl.ds(t * G, G)
        local = bh[rows, mine].astype(jnp.float32) + bl[rows, mine].astype(jnp.float32)
        turned = local.T * potential[t : t + 1, :]
        high, low = split(turned)
        wh[:, t * G : (t + 1) * G] = high
        wl[:, t * G : (t + 1) * G] = low
    half = lane_half()
    square = jnp.broadcast_to(sums[tiles : tiles + 1, 0:1], (8, lanes))

    @pl.loop(0, row_count)
    def _(r):
        at = pl.ds(pl.multiple_of(r * lanes, PAIR), lanes)
        chunk[...] = dot3(wh[...], wl[...], bh[:, at], bl[:, at])
        for pair in range(lanes // PAIR):
            l = r * (lanes // BS) + 2 * pair
            here = slice(pair * PAIR, (pair + 1) * PAIR)
            for s in range(ks_slots):
                left = pl.ds(pl.multiple_of(ks[l, s] * BS, BS), BS)
                right = pl.ds(pl.multiple_of(ks[l + 1, s] * BS, BS), BS)
                out[r, s * BS : (s + 1) * BS, here] = jnp.where(
                    half == 0.0, chunk[left, here], chunk[right, here]
                )
        out[r, out_rows - 8 : out_rows, :] = square


def plain(
    density_values, density_cols, ks_cols, core_hamiltonian, tile_blocks, grid_weights, basis_values
):
    highest = lax.Precision.HIGHEST
    row_blocks, own_slots = density_cols.shape
    ks_slots = ks_cols.shape[1]
    panel, panel_cols, panel_ks = (
        lax.all_gather(density_values, "row", axis=0, tiled=True),
        lax.all_gather(density_cols, "row", axis=0, tiled=True),
        lax.all_gather(ks_cols, "row", axis=0, tiled=True),
    )
    all_blocks = panel_cols.shape[0]
    panel_blocks = panel.reshape(all_blocks, BS, own_slots, BS)
    empty = jnp.zeros((row_blocks, BS, own_slots, BS), jnp.float32)
    values = lax.all_gather(density_values, "col", axis=1, tiled=True)
    columns = lax.all_gather(density_cols, "col", axis=1, tiled=True)
    width = columns.shape[1]
    left_blocks = values.reshape(row_blocks, BS, width, BS)
    neighbours = panel_blocks[columns]
    their_cols = panel_cols[columns]
    matches = (their_cols[:, :, :, None] == density_cols[:, None, None, :]).astype(jnp.float32)
    combined = jnp.einsum("ipqr,ipaqh->iprah", matches, neighbours, precision=highest)
    product = empty + jnp.einsum("ifpa,iprah->ifrh", left_blocks, combined, precision=highest)
    kept = product.reshape(row_blocks * BS, own_slots * BS)
    total_square = lax.psum(jnp.sum(kept * kept), ("row", "col"))
    entry_count = all_blocks * BS * own_slots * lax.axis_size("col") * BS
    purified = kept / jnp.sqrt(total_square / entry_count + 1e-06)
    tile_count = tile_blocks.shape[0]
    basis = basis_values.reshape(tile_count, G, TB, BS)
    tile_rows = panel_blocks[tile_blocks]
    tile_cols = panel_cols[tile_blocks]
    halves = jnp.einsum("tgif,tifqh->tgiqh", basis, tile_rows, precision=highest)
    matches = (tile_cols[:, :, :, None] == tile_blocks[:, None, None, :]).astype(jnp.float32)
    combined = jnp.einsum("tiqj,tgiqh->tgjh", matches, halves, precision=highest)
    partial_density = jnp.sum(combined * basis, axis=(2, 3))
    grid_density = lax.psum(partial_density, "col")
    potential = grid_weights * jnp.tanh(grid_density)
    weighted = basis * potential[:, :, None, None]
    ks_here = panel_ks[tile_blocks]
    ks_matches = (ks_here[:, :, :, None] == tile_blocks[:, None, None, :]).astype(jnp.float32)
    selected = jnp.einsum("tisj,tgjh->tgish", ks_matches, basis, precision=highest)
    pairs = jnp.einsum("tgif,tgish->tifsh", weighted, selected, precision=highest)
    ks_panel = jnp.zeros((all_blocks, BS, ks_slots, BS), jnp.float32)
    ks_panel = ks_panel.at[tile_blocks.reshape(-1)].add(
        pairs.reshape(tile_count * TB, BS, ks_slots, BS)
    )
    own_rows = lax.psum_scatter(
        ks_panel.reshape(all_blocks * BS, ks_slots * BS), "row", scatter_dimension=0, tiled=True
    )
    kohn_sham = core_hamiltonian + own_rows
    return (kohn_sham, purified)


def dense(
    density_values, density_cols, ks_cols, core_hamiltonian, tile_blocks, grid_weights, basis_values
):
    row_blocks, own_slots = density_cols.shape
    ks_slots = ks_cols.shape[1]
    row_count, col_count = lax.axis_size("row"), lax.axis_size("col")
    all_blocks = row_blocks * row_count
    col_blocks = all_blocks // col_count
    width = col_blocks * BS
    order = all_blocks * BS
    tiles = tile_blocks.shape[0]
    points = tiles * G
    rows = row_blocks * BS
    col = lax.axis_index("col")
    f32, bf16 = jnp.float32, jnp.bfloat16
    vmem, smem = pl.BlockSpec(memory_space=pltpu.VMEM), pl.BlockSpec(memory_space=pltpu.SMEM)
    params = pltpu.CompilerParams(vmem_limit_bytes=VMEM_BUDGET)

    local_codes = jnp.repeat((density_cols - col * col_blocks).astype(f32), BS, axis=1)
    local_ks = (ks_cols - col * col_blocks).astype(f32)
    ks_lines = jnp.pad(local_ks, ((0, 0), (0, PAIR - ks_slots)))
    extra = 2 * row_blocks
    packed = jnp.concatenate([density_values, local_codes, ks_lines], axis=0)
    by_row = lax.all_gather(packed, "row", axis=0)
    by_col = lax.all_gather(packed, "col", axis=0)

    blocks = jnp.arange(all_blocks, dtype=jnp.int32)
    index = jnp.arange(TB, dtype=jnp.int32)
    same = tile_blocks[:, :, None] == blocks[None, None, :]
    places = jnp.min(jnp.where(same, index[None, :, None], TB), axis=1).astype(jnp.int32)
    here = jnp.reshape(col, (1,)).astype(jnp.int32)

    bh, bl = pl.pallas_call(
        expand_kernel,
        out_shape=[jax.ShapeDtypeStruct((points, order), bf16)] * 2,
        in_specs=[smem, vmem],
        out_specs=[vmem, vmem],
        scratch_shapes=[pltpu.VMEM((2, TB // 2 + 1, G, PAIR), f32)],
        compiler_params=params,
        cost_estimate=pl.CostEstimate(
            flops=0, bytes_accessed=4 * points * order + 4 * points * TB * BS, transcendentals=0
        ),
        name="expand_basis",
    )(places, basis_values)

    panel = by_row[:, :rows].reshape(order, PAIR)
    codes = by_row[:, rows : rows + row_blocks].reshape(all_blocks, PAIR)
    ks_all = by_row[:, rows + row_blocks :, :ks_slots].reshape(all_blocks, ks_slots)
    ks_all = ks_all.astype(jnp.int32)
    own = by_col[:, :rows]
    own_codes = by_col[:, rows : rows + row_blocks]
    parts, kept = pl.pallas_call(
        density_kernel,
        out_shape=[
            jax.ShapeDtypeStruct((tiles + 8, PAIR), f32),
            jax.ShapeDtypeStruct((rows, PAIR), f32),
        ],
        in_specs=[smem] + [vmem] * 7,
        out_specs=[vmem, vmem],
        scratch_shapes=[pltpu.VMEM((order, width), bf16)] * 2 + [pltpu.VMEM((rows, order), bf16)] * 2,
        compiler_params=params,
        cost_estimate=pl.CostEstimate(
            flops=6 * points * order * width, bytes_accessed=4 * points * order, transcendentals=0
        ),
        name="grid_density",
    )(here, bh, bl, panel, codes, own, own_codes, local_codes)
    sums = lax.psum(parts, "col")

    contributions = pl.pallas_call(
        exchange_kernel,
        out_shape=jax.ShapeDtypeStruct((row_count, ks_slots * BS + 8, rows), f32),
        in_specs=[smem, smem] + [vmem] * 4,
        out_specs=vmem,
        scratch_shapes=[pltpu.VMEM((width, points), bf16)] * 2 + [pltpu.VMEM((width, rows), f32)],
        compiler_params=params,
        cost_estimate=pl.CostEstimate(
            flops=6 * points * order * width, bytes_accessed=4 * points * order, transcendentals=0
        ),
        name="exchange",
    )(here, ks_all, bh, bl, sums, grid_weights)
    mine = lax.psum_scatter(contributions, "row", scatter_dimension=0, tiled=False)
    kohn_sham = core_hamiltonian + mine[: ks_slots * BS].T
    entry_count = order * own_slots * col_count * BS
    purified = kept / jnp.sqrt(mine[ks_slots * BS, 0] / entry_count + 1e-06)
    return (kohn_sham, purified)


def on_device(*args):
    density_cols, tile_blocks = args[1], args[4]
    all_blocks = density_cols.shape[0] * lax.axis_size("row")
    order = all_blocks * BS
    width = order // lax.axis_size("col")
    points = tile_blocks.shape[0] * G
    held = 4 * points * order + 4 * order * width + 4 * points * TB * BS
    fits = held + 8 * points * width < VMEM_BUDGET
    regular = density_cols.shape[1] * BS == PAIR and density_cols.shape[0] % 4 == 0
    if fits and regular and width % PAIR == 0 and tile_blocks.shape[0] % 8 == 0:
        return dense(*args)
    return plain(*args)


def solution(mesh):
    in_specs = (
        P("row", "col"),
        P("row", "col"),
        P("row", "col"),
        P("row", "col"),
        P("row", None),
        P("row", None),
        P("row", None, None),
    )
    out_specs = (P("row", "col"), P("row", "col"))
    return jax.shard_map(
        on_device, mesh=mesh, in_specs=in_specs, out_specs=out_specs, check_vma=False
    )
```

```python
import functools
import jax
import jax.numpy as jnp
from jax import lax
from jax.experimental import pallas as pl
from jax.experimental.pallas import tpu as pltpu
from jax.sharding import PartitionSpec as P

BS = 64
TB = 16
G = 128
PAIR = 2 * BS
VMEM_BUDGET = 52 * 1024 * 1024


def split(x):
    high = x.astype(jnp.bfloat16)
    return high, (x - high.astype(jnp.float32)).astype(jnp.bfloat16)


def dot(a, b):
    return jnp.dot(a, b, preferred_element_type=jnp.float32)


def dot3(ah, al, bh, bl):
    return dot(ah, bh) + (dot(ah, bl) + dot(al, bh))


def lane_half():
    return (lax.broadcasted_iota(jnp.int32, (1, PAIR), 1) >= BS).astype(jnp.float32)


def widen(values, codes, out_h, out_l, row, first_lane, pairs):
    half = lane_half()
    swapped = pltpu.roll(values, BS, 1)
    swapped_codes = pltpu.roll(jnp.broadcast_to(codes, (8, PAIR)), BS, 1)[0:1]
    for p in range(pairs):
        block = 2.0 * p + half
        dense = jnp.where(codes == block, values, 0.0) + jnp.where(
            swapped_codes == block, swapped, 0.0
        )
        high, low = split(dense)
        lanes = pl.ds(first_lane + p * PAIR, PAIR)
        out_h[pl.ds(row, BS), lanes] = high
        out_l[pl.ds(row, BS), lanes] = low


MESH = pl.DeviceIdType.MESH


def mega_kernel(
    places, basis, packed, weights, core,
    kohn, purified,
    bh, bl, sources, by_row, by_col, dh, dl, oh, ol, product, kept, parts_out, parts_in, turned, wh, wl,
    chunk, pair_out, pair_in, mid, line_in,
    row_send, row_recv, pass_send, col_send, col_recv, part_send, part_recv,
    pair_send, pair_recv, line_send, line_recv,
    *, row_blocks, ks_slots, entry_count,
):
    row_count, col_count = by_row.shape[0], by_col.shape[0]
    row, col = lax.axis_index("row"), lax.axis_index("col")
    side, place = row % 2, row // 2
    line = row_count // 2
    partner = 2 * place + 1 - side
    rows = row_blocks * BS
    tiles = basis.shape[0]
    points = tiles * G
    width = dh.shape[1]
    pairs = width // PAIR
    half = lane_half()

    def on_line(d):
        return 2 * lax.rem(place + d, line) + side

    def col_at(d):
        return lax.rem(col + d, col_count)

    def remote(src, dst, send, recv, to_row, to_col):
        return pltpu.make_async_remote_copy(
            src_ref=src, dst_ref=dst, send_sem=send, recv_sem=recv,
            device_id=(to_row, to_col), device_id_type=MESH,
        )

    barrier = pltpu.get_barrier_semaphore()
    pl.semaphore_signal(barrier, inc=1, device_id=(partner, col), device_id_type=MESH)
    for d in range(1, line):
        pl.semaphore_signal(barrier, inc=1, device_id=(on_line(d), col), device_id_type=MESH)
    for d in range(1, col_count):
        pl.semaphore_signal(barrier, inc=1, device_id=(row, col_at(d)), device_id_type=MESH)
    pl.semaphore_wait(barrier, line + col_count - 1)

    own_sends = []
    for d in range(1, line):
        own_sends.append(
            remote(packed, by_row.at[row], row_send.at[d], row_recv.at[row], on_line(d), col)
        )
    own_sends.append(remote(packed, by_row.at[row], row_send.at[0], row_recv.at[row], partner, col))
    for d in range(1, col_count):
        own_sends.append(
            remote(packed, by_col.at[col], col_send.at[d], col_recv.at[col], row, col_at(d))
        )
    for copy in own_sends:
        copy.start()
    by_row[row] = packed[...]
    by_col[col] = packed[...]

    source_pairs = basis.shape[2] // PAIR
    sources[0, source_pairs] = jnp.zeros((G, PAIR), jnp.float32)
    sources[1, source_pairs] = jnp.zeros((G, PAIR), jnp.float32)

    def expand(t):
        for p in range(source_pairs):
            x = basis[t, :, p * PAIR : (p + 1) * PAIR]
            sources[0, p] = x
            sources[1, p] = pltpu.roll(x, BS, 1)
        at = pl.ds(pl.multiple_of(t * G, G), G)
        for d in range(bh.shape[1] // PAIR):
            left = places[t, 2 * d]
            right = places[t, 2 * d + 1]
            dense = jnp.where(
                half == 0.0,
                sources[left % 2, left // 2],
                sources[1 - right % 2, right // 2],
            )
            high, low = split(dense)
            bh[at, d * PAIR : (d + 1) * PAIR] = high
            bl[at, d * PAIR : (d + 1) * PAIR] = low

    pl.loop(0, tiles // 2)(expand)

    passed = []
    for d in range(1, line):
        origin = 2 * lax.rem(place + line - d, line) + side
        remote(
            packed, by_row.at[origin], row_send.at[d], row_recv.at[origin], partner, col
        ).wait_recv()
        copy = remote(
            by_row.at[origin], by_row.at[origin], pass_send.at[d], row_recv.at[origin], partner, col
        )
        copy.start()
        passed.append(copy)

    pl.loop(tiles // 2, tiles)(expand)

    for d in range(1, col_count):
        origin = col_at(d)
        remote(
            packed, by_col.at[origin], col_send.at[d], col_recv.at[origin], row, origin
        ).wait_recv()
    for d in range(line):
        origin = 2 * lax.rem(place + line - d, line) + 1 - side
        remote(
            packed, by_row.at[origin], row_send.at[0], row_recv.at[origin], partner, col
        ).wait_recv()

    def widen_row(r):
        for l in range(row_blocks):
            at = pl.multiple_of((r * row_blocks + l) * BS, BS)
            widen(
                by_row[r, l * BS : (l + 1) * BS, :],
                by_row[r, rows + l : rows + l + 1, :],
                dh, dl, at, 0, pairs,
            )

    pl.loop(0, row_count)(widen_row)
    for c in range(col_count):
        for l in range(row_blocks):
            widen(
                by_col[c, l * BS : (l + 1) * BS, :],
                by_col[c, rows + l : rows + l + 1, :],
                oh, ol, l * BS, c * width, pairs,
            )

    step = 4 * G
    mine = pl.ds(pl.multiple_of(col * width, PAIR), width)

    @pl.loop(0, points // step)
    def _(s):
        at = pl.ds(pl.multiple_of(s * step, step), step)
        x = dot3(bh[at, :], bl[at, :], dh[...], dl[...])
        local = bh[at, mine].astype(jnp.float32) + bl[at, mine].astype(jnp.float32)
        sums = jnp.sum(x * local, axis=1, keepdims=True)
        for t in range(step // G):
            tile = jnp.broadcast_to(sums[t * G : (t + 1) * G], (G, G))
            parts_out[pl.ds(s * (step // G) + t, 1), :] = tile.T[0:1, :]

    product[...] = dot3(oh[...], ol[...], dh[...], dl[...])
    total = jnp.zeros((BS, PAIR), jnp.float32)
    for l in range(row_blocks):
        codes_here = packed[rows + l : rows + l + 1, :]
        block = jnp.zeros((BS, PAIR), jnp.float32)
        for p in range(pairs):
            piece = product[l * BS : (l + 1) * BS, p * PAIR : (p + 1) * PAIR]
            block += jnp.where(codes_here == 2.0 * p + half, piece, 0.0)
            block += jnp.where(
                codes_here == 2.0 * p + 1.0 - half, pltpu.roll(piece, BS, 1), 0.0
            )
        kept[l * BS : (l + 1) * BS, :] = block
        total += block * block
    square = jnp.sum(jnp.sum(total, axis=1, keepdims=True), axis=0, keepdims=True)
    parts_out[tiles : tiles + 8, :] = jnp.broadcast_to(square, (8, PAIR))

    part_sends = []
    for d in range(1, col_count):
        copy = remote(
            parts_out, parts_in.at[col], part_send.at[d], part_recv.at[col], row, col_at(d)
        )
        copy.start()
        part_sends.append(copy)
    parts_in[col] = parts_out[...]
    for t in range(tiles):
        at = pl.ds(t * G, G)
        local = bh[at, mine].astype(jnp.float32) + bl[at, mine].astype(jnp.float32)
        turned[:, t * G : (t + 1) * G] = local.T
    for d in range(1, col_count):
        origin = col_at(d)
        remote(
            parts_out, parts_in.at[origin], part_send.at[d], part_recv.at[origin], row, origin
        ).wait_recv()
    sums = parts_in[0]
    for c in range(1, col_count):
        sums += parts_in[c]
    potential = weights[...] * jnp.tanh(sums[0:tiles, :])
    for t in range(tiles):
        high, low = split(turned[:, t * G : (t + 1) * G] * potential[t : t + 1, :])
        wh[:, t * G : (t + 1) * G] = high
        wl[:, t * G : (t + 1) * G] = low
    lanes = core.shape[0]
    stored = ks_slots * BS
    square_all = jnp.broadcast_to(sums[tiles : tiles + 1, 0:1], (8, lanes))

    def contribute(owner, out, i):
        at = pl.ds(pl.multiple_of(owner * lanes, PAIR), lanes)
        chunk[...] = dot3(wh[...], wl[...], bh[:, at], bl[:, at])
        for h in range(lanes // PAIR):
            here = slice(h * PAIR, (h + 1) * PAIR)
            for s in range(ks_slots):
                line_at = rows + row_blocks + h * ks_slots + s
                code = by_row[owner, line_at : line_at + 1, :]
                block = jnp.zeros((BS, PAIR), jnp.float32)
                for k in range(width // BS):
                    block += jnp.where(code == float(k), chunk[k * BS : (k + 1) * BS, here], 0.0)
                out[i, s * BS : (s + 1) * BS, here] = block
        out[i, stored : stored + 8, :] = square_all

    def pair_copy(i):
        return remote(
            pair_out.at[i], pair_in.at[i], pair_send.at[i], pair_recv.at[i], partner, col
        )

    def line_copy(i):
        return remote(
            mid.at[i], line_in.at[i], line_send.at[i], line_recv.at[i], on_line(i + 1), col
        )

    def join(i):
        pair_copy(i).wait_recv()
        mid[i] = mid[i] + pair_in[i]

    @pl.loop(0, line)
    def _(i):
        owner = on_line(i + 1)
        contribute(owner + 1 - 2 * side, pair_out, i)
        pair_copy(i).start()
        contribute(owner, mid, i)

        @pl.when(i >= 1)
        def _():
            join(i - 1)
            line_copy(i - 1).start()

    join(line - 1)
    result = mid[line - 1]
    for i in range(line - 1):
        line_copy(i).wait_recv()
        result += line_in[i]
    kohn[...] = core[...] + result[0:stored, :].T
    mean_square = result[stored : stored + 1, 0:1] / entry_count
    purified[...] = kept[...] / jnp.sqrt(mean_square + 1e-06)

    for copy in own_sends + passed + part_sends:
        copy.wait_send()
    for i in range(line):
        pair_copy(i).wait_send()
    for i in range(line - 1):
        line_copy(i).wait_send()


def plain(
    density_values, density_cols, ks_cols, core_hamiltonian, tile_blocks, grid_weights, basis_values
):
    highest = lax.Precision.HIGHEST
    row_blocks, own_slots = density_cols.shape
    ks_slots = ks_cols.shape[1]
    panel, panel_cols, panel_ks = (
        lax.all_gather(density_values, "row", axis=0, tiled=True),
        lax.all_gather(density_cols, "row", axis=0, tiled=True),
        lax.all_gather(ks_cols, "row", axis=0, tiled=True),
    )
    all_blocks = panel_cols.shape[0]
    panel_blocks = panel.reshape(all_blocks, BS, own_slots, BS)
    empty = jnp.zeros((row_blocks, BS, own_slots, BS), jnp.float32)
    values = lax.all_gather(density_values, "col", axis=1, tiled=True)
    columns = lax.all_gather(density_cols, "col", axis=1, tiled=True)
    width = columns.shape[1]
    left_blocks = values.reshape(row_blocks, BS, width, BS)
    neighbours = panel_blocks[columns]
    their_cols = panel_cols[columns]
    matches = (their_cols[:, :, :, None] == density_cols[:, None, None, :]).astype(jnp.float32)
    combined = jnp.einsum("ipqr,ipaqh->iprah", matches, neighbours, precision=highest)
    product = empty + jnp.einsum("ifpa,iprah->ifrh", left_blocks, combined, precision=highest)
    kept = product.reshape(row_blocks * BS, own_slots * BS)
    total_square = lax.psum(jnp.sum(kept * kept), ("row", "col"))
    entry_count = all_blocks * BS * own_slots * lax.axis_size("col") * BS
    purified = kept / jnp.sqrt(total_square / entry_count + 1e-06)
    tile_count = tile_blocks.shape[0]
    basis = basis_values.reshape(tile_count, G, TB, BS)
    tile_rows = panel_blocks[tile_blocks]
    tile_cols = panel_cols[tile_blocks]
    halves = jnp.einsum("tgif,tifqh->tgiqh", basis, tile_rows, precision=highest)
    matches = (tile_cols[:, :, :, None] == tile_blocks[:, None, None, :]).astype(jnp.float32)
    combined = jnp.einsum("tiqj,tgiqh->tgjh", matches, halves, precision=highest)
    partial_density = jnp.sum(combined * basis, axis=(2, 3))
    grid_density = lax.psum(partial_density, "col")
    potential = grid_weights * jnp.tanh(grid_density)
    weighted = basis * potential[:, :, None, None]
    ks_here = panel_ks[tile_blocks]
    ks_matches = (ks_here[:, :, :, None] == tile_blocks[:, None, None, :]).astype(jnp.float32)
    selected = jnp.einsum("tisj,tgjh->tgish", ks_matches, basis, precision=highest)
    pairs = jnp.einsum("tgif,tgish->tifsh", weighted, selected, precision=highest)
    ks_panel = jnp.zeros((all_blocks, BS, ks_slots, BS), jnp.float32)
    ks_panel = ks_panel.at[tile_blocks.reshape(-1)].add(
        pairs.reshape(tile_count * TB, BS, ks_slots, BS)
    )
    own_rows = lax.psum_scatter(
        ks_panel.reshape(all_blocks * BS, ks_slots * BS), "row", scatter_dimension=0, tiled=True
    )
    kohn_sham = core_hamiltonian + own_rows
    return (kohn_sham, purified)


def dense(
    density_values, density_cols, ks_cols, core_hamiltonian, tile_blocks, grid_weights, basis_values
):
    row_blocks, own_slots = density_cols.shape
    ks_slots = ks_cols.shape[1]
    row_count, col_count = lax.axis_size("row"), lax.axis_size("col")
    all_blocks = row_blocks * row_count
    col_blocks = all_blocks // col_count
    width = col_blocks * BS
    order = all_blocks * BS
    tiles = tile_blocks.shape[0]
    points = tiles * G
    rows = row_blocks * BS
    line = row_count // 2
    stored = ks_slots * BS
    col = lax.axis_index("col")
    f32, bf16 = jnp.float32, jnp.bfloat16
    vmem, smem = pl.BlockSpec(memory_space=pltpu.VMEM), pl.BlockSpec(memory_space=pltpu.SMEM)

    local_codes = jnp.repeat((density_cols - col * col_blocks).astype(f32), BS, axis=1)
    local_ks = jnp.repeat((ks_cols - col * col_blocks).astype(f32).T, BS, axis=1)
    ks_lines = [local_ks[:, at : at + PAIR] for at in range(0, rows, PAIR)]
    used = rows + row_blocks + ks_slots * (rows // PAIR)
    fill = jnp.zeros((-used % 16, PAIR), f32)
    packed = jnp.concatenate([density_values, local_codes, *ks_lines, fill], axis=0)

    blocks = jnp.arange(all_blocks, dtype=jnp.int32)
    index = jnp.arange(TB, dtype=jnp.int32)
    same = tile_blocks[:, :, None] == blocks[None, None, :]
    places = jnp.min(jnp.where(same, index[None, :, None], TB), axis=1).astype(jnp.int32)

    dma = pltpu.SemaphoreType.DMA
    kernel = functools.partial(
        mega_kernel,
        row_blocks=row_blocks,
        ks_slots=ks_slots,
        entry_count=float(order * own_slots * col_count * BS),
    )
    packed_rows = packed.shape[0]
    return tuple(
        pl.pallas_call(
            kernel,
            out_shape=[
                jax.ShapeDtypeStruct((rows, stored), f32),
                jax.ShapeDtypeStruct((rows, PAIR), f32),
            ],
            in_specs=[smem] + [vmem] * 4,
            out_specs=[vmem, vmem],
            scratch_shapes=[
                pltpu.VMEM((points, order), bf16),
                pltpu.VMEM((points, order), bf16),
                pltpu.VMEM((2, TB // 2 + 1, G, PAIR), f32),
                pltpu.VMEM((row_count, packed_rows, PAIR), f32),
                pltpu.VMEM((col_count, packed_rows, PAIR), f32),
                pltpu.VMEM((order, width), bf16),
                pltpu.VMEM((order, width), bf16),
                pltpu.VMEM((rows, order), bf16),
                pltpu.VMEM((rows, order), bf16),
                pltpu.VMEM((rows, width), f32),
                pltpu.VMEM((rows, PAIR), f32),
                pltpu.VMEM((tiles + 8, PAIR), f32),
                pltpu.VMEM((col_count, tiles + 8, PAIR), f32),
                pltpu.VMEM((width, points), f32),
                pltpu.VMEM((width, points), bf16),
                pltpu.VMEM((width, points), bf16),
                pltpu.VMEM((width, rows), f32),
                pltpu.VMEM((line, stored + 8, rows), f32),
                pltpu.VMEM((line, stored + 8, rows), f32),
                pltpu.VMEM((line, stored + 8, rows), f32),
                pltpu.VMEM((line, stored + 8, rows), f32),
                dma((line,)),
                dma((row_count,)),
                dma((line,)),
                dma((col_count,)),
                dma((col_count,)),
                dma((col_count,)),
                dma((col_count,)),
                dma((line,)),
                dma((line,)),
                dma((line,)),
                dma((line,)),
            ],
            compiler_params=pltpu.CompilerParams(
                vmem_limit_bytes=VMEM_BUDGET, collective_id=0, has_side_effects=True
            ),
            cost_estimate=pl.CostEstimate(
                flops=12 * points * order * width,
                bytes_accessed=4 * points * TB * BS,
                transcendentals=points,
            ),
            name="kohn_sham_build",
        )(places, basis_values, packed, grid_weights, core_hamiltonian)
    )


def on_device(*args):
    density_cols, tile_blocks = args[1], args[4]
    all_blocks = density_cols.shape[0] * lax.axis_size("row")
    order = all_blocks * BS
    width = order // lax.axis_size("col")
    points = tile_blocks.shape[0] * G
    held = 4 * points * order + 4 * order * width + 4 * points * TB * BS
    fits = held + 16 * points * width < VMEM_BUDGET
    regular = density_cols.shape[1] * BS == PAIR and density_cols.shape[0] % 2 == 0
    regular = regular and lax.axis_size("row") % 2 == 0
    if fits and regular and width % PAIR == 0 and tile_blocks.shape[0] % 8 == 0:
        return dense(*args)
    return plain(*args)


def solution(mesh):
    in_specs = (
        P("row", "col"),
        P("row", "col"),
        P("row", "col"),
        P("row", "col"),
        P("row", None),
        P("row", None),
        P("row", None, None),
    )
    out_specs = (P("row", "col"), P("row", "col"))
    return jax.shard_map(
        on_device, mesh=mesh, in_specs=in_specs, out_specs=out_specs, check_vma=False
    )
```

```python
import functools
import jax
import jax.numpy as jnp
from jax import lax
from jax.experimental import pallas as pl
from jax.experimental.pallas import tpu as pltpu
from jax.sharding import PartitionSpec as P

BS = 64
TB = 16
G = 128
PAIR = 2 * BS
VMEM_BUDGET = 52 * 1024 * 1024


def split(x):
    high = x.astype(jnp.bfloat16)
    return high, (x - high.astype(jnp.float32)).astype(jnp.bfloat16)


def dot(a, b):
    return jnp.dot(a, b, preferred_element_type=jnp.float32)


def dot3(ah, al, bh, bl):
    return dot(ah, bh) + (dot(ah, bl) + dot(al, bh))


def lane_half():
    return (lax.broadcasted_iota(jnp.int32, (1, PAIR), 1) >= BS).astype(jnp.float32)


def widen(values, codes, out_h, out_l, row, first_lane, pairs):
    half = lane_half()
    swapped = pltpu.roll(values, BS, 1)
    swapped_codes = pltpu.roll(jnp.broadcast_to(codes, (8, PAIR)), BS, 1)[0:1]
    for p in range(pairs):
        block = 2.0 * p + half
        dense = jnp.where(codes == block, values, 0.0) + jnp.where(
            swapped_codes == block, swapped, 0.0
        )
        high, low = split(dense)
        lanes = pl.ds(first_lane + p * PAIR, PAIR)
        out_h[pl.ds(row, BS), lanes] = high
        out_l[pl.ds(row, BS), lanes] = low


MESH = pl.DeviceIdType.MESH


def mega_kernel(
    places, density_cols, ks_cols, basis_hbm, values, weights, core,
    kohn, purified,
    basis, packed, acc, square_out, square_in, bh, bl, sources, by_row, by_col, dh, dl, oh, ol, product, kept, parts_out, parts_in, turned, wh, wl,
    chunk, pair_out, pair_in, mid, line_in,
    row_send, row_recv, pass_send, col_send, col_recv, part_send, part_recv,
    pair_send, pair_recv, line_send, line_recv, square_send, square_recv, basis_sem,
    *, row_blocks, ks_slots, entry_count,
):
    row_count, col_count = by_row.shape[0], by_col.shape[0]
    row, col = lax.axis_index("row"), lax.axis_index("col")
    side, place = row % 2, row // 2
    line = row_count // 2
    partner = 2 * place + 1 - side
    rows = row_blocks * BS
    tiles = basis.shape[0]
    points = tiles * G
    width = dh.shape[1]
    pairs = width // PAIR
    half = lane_half()

    def on_line(d):
        return 2 * lax.rem(place + d, line) + side

    def col_at(d):
        return lax.rem(col + d, col_count)

    def remote(src, dst, send, recv, to_row, to_col):
        return pltpu.make_async_remote_copy(
            src_ref=src, dst_ref=dst, send_sem=send, recv_sem=recv,
            device_id=(to_row, to_col), device_id_type=MESH,
        )

    load_basis = pltpu.make_async_copy(basis_hbm, basis, basis_sem)
    load_basis.start()
    barrier = pltpu.get_barrier_semaphore()
    pl.semaphore_signal(barrier, inc=1, device_id=(partner, col), device_id_type=MESH)
    for d in range(1, line):
        pl.semaphore_signal(barrier, inc=1, device_id=(on_line(d), col), device_id_type=MESH)
    for d in range(1, col_count):
        pl.semaphore_signal(barrier, inc=1, device_id=(row, col_at(d)), device_id_type=MESH)
    base = col * (width // BS)

    def code_line(left, right):
        both = jnp.where(half == 0.0, left - base, right - base)
        return both.astype(jnp.float32)

    packed[0:rows, :] = values[...]
    for l in range(row_blocks):
        packed[rows + l : rows + l + 1, :] = code_line(density_cols[l, 0], density_cols[l, 1])
    used = rows + row_blocks
    for h in range(row_blocks // 2):
        for slot in range(ks_slots):
            packed[used : used + 1, :] = code_line(ks_cols[2 * h, slot], ks_cols[2 * h + 1, slot])
            used += 1
    if used < packed.shape[0]:
        packed[used:, :] = jnp.zeros((packed.shape[0] - used, PAIR), jnp.float32)
    pl.semaphore_wait(barrier, line + col_count - 1)

    own_sends = []
    for d in range(1, line):
        own_sends.append(
            remote(packed, by_row.at[row], row_send.at[d], row_recv.at[row], on_line(d), col)
        )
    own_sends.append(remote(packed, by_row.at[row], row_send.at[0], row_recv.at[row], partner, col))
    for d in range(1, col_count):
        own_sends.append(
            remote(packed, by_col.at[col], col_send.at[d], col_recv.at[col], row, col_at(d))
        )
    for copy in own_sends:
        copy.start()
    by_row[row] = packed[...]
    by_col[col] = packed[...]

    source_pairs = basis.shape[2] // PAIR
    sources[0, source_pairs] = jnp.zeros((G, PAIR), jnp.float32)
    sources[1, source_pairs] = jnp.zeros((G, PAIR), jnp.float32)

    def expand(t):
        for p in range(source_pairs):
            x = basis[t, :, p * PAIR : (p + 1) * PAIR]
            sources[0, p] = x
            sources[1, p] = pltpu.roll(x, BS, 1)
        at = pl.ds(pl.multiple_of(t * G, G), G)
        for d in range(bh.shape[1] // PAIR):
            left = places[t, 2 * d]
            right = places[t, 2 * d + 1]
            dense = jnp.where(
                half == 0.0,
                sources[left % 2, left // 2],
                sources[1 - right % 2, right // 2],
            )
            high, low = split(dense)
            bh[at, d * PAIR : (d + 1) * PAIR] = high
            bl[at, d * PAIR : (d + 1) * PAIR] = low

    acc[...] = jnp.zeros(acc.shape, jnp.float32)
    load_basis.wait()
    cuts = [tiles * d // line for d in range(line + 1)]
    pl.loop(cuts[0], cuts[1])(expand)

    passed = []
    for d in range(1, line):
        origin = 2 * lax.rem(place + line - d, line) + side
        remote(
            packed, by_row.at[origin], row_send.at[d], row_recv.at[origin], partner, col
        ).wait_recv()
        copy = remote(
            by_row.at[origin], by_row.at[origin], pass_send.at[d], row_recv.at[origin], partner, col
        )
        copy.start()
        passed.append(copy)
        pl.loop(cuts[d], cuts[d + 1])(expand)

    def widen_row(r):
        for l in range(row_blocks):
            at = pl.multiple_of((r * row_blocks + l) * BS, BS)
            widen(
                by_row[r, l * BS : (l + 1) * BS, :],
                by_row[r, rows + l : rows + l + 1, :],
                dh, dl, at, 0, pairs,
            )

    step = 4 * G

    def absorb(r):
        widen_row(r)
        deep = pl.ds(pl.multiple_of(r * rows, PAIR), rows)

        @pl.loop(0, points // step)
        def _(s):
            at = pl.ds(pl.multiple_of(s * step, step), step)
            acc[at, :] += dot3(bh[at, deep], bl[at, deep], dh[deep, :], dl[deep, :])

    @pl.loop(0, line)
    def _(d):
        absorb(on_line(d))

    @pl.loop(0, line)
    def _(d):
        origin = 2 * lax.rem(place + line - d, line) + 1 - side
        remote(
            packed, by_row.at[origin], row_send.at[0], row_recv.at[origin], partner, col
        ).wait_recv()
        absorb(origin)

    mine = pl.ds(pl.multiple_of(col * width, PAIR), width)

    @pl.loop(0, tiles)
    def _(t):
        at = pl.ds(pl.multiple_of(t * G, G), G)
        local = bh[at, mine].astype(jnp.float32) + bl[at, mine].astype(jnp.float32)
        sums = jnp.sum(acc[at, :] * local, axis=1, keepdims=True)
        parts_out[pl.ds(t, 1), :] = jnp.broadcast_to(sums, (G, G)).T[0:1, :]

    part_sends = []
    for d in range(1, col_count):
        copy = remote(
            parts_out, parts_in.at[col], part_send.at[d], part_recv.at[col], row, col_at(d)
        )
        copy.start()
        part_sends.append(copy)
    parts_in[col] = parts_out[...]

    for d in range(1, col_count):
        origin = col_at(d)
        remote(
            packed, by_col.at[origin], col_send.at[d], col_recv.at[origin], row, origin
        ).wait_recv()
    for c in range(col_count):
        for l in range(row_blocks):
            widen(
                by_col[c, l * BS : (l + 1) * BS, :],
                by_col[c, rows + l : rows + l + 1, :],
                oh, ol, l * BS, c * width, pairs,
            )
    product[...] = dot3(oh[...], ol[...], dh[...], dl[...])
    total = jnp.zeros((BS, PAIR), jnp.float32)
    for l in range(row_blocks):
        codes_here = packed[rows + l : rows + l + 1, :]
        block = jnp.zeros((BS, PAIR), jnp.float32)
        for p in range(pairs):
            piece = product[l * BS : (l + 1) * BS, p * PAIR : (p + 1) * PAIR]
            block += jnp.where(codes_here == 2.0 * p + half, piece, 0.0)
            block += jnp.where(
                codes_here == 2.0 * p + 1.0 - half, pltpu.roll(piece, BS, 1), 0.0
            )
        kept[l * BS : (l + 1) * BS, :] = block
        total += block * block
    square = jnp.sum(jnp.sum(total, axis=1, keepdims=True), axis=0, keepdims=True)
    square_out[...] = jnp.broadcast_to(square, (8, PAIR))
    for d in range(1, col_count):
        copy = remote(
            square_out, square_in.at[col], square_send.at[d], square_recv.at[col], row, col_at(d)
        )
        copy.start()
        part_sends.append(copy)
    square_in[col] = square_out[...]
    for t in range(tiles):
        at = pl.ds(t * G, G)
        local = bh[at, mine].astype(jnp.float32) + bl[at, mine].astype(jnp.float32)
        turned[:, t * G : (t + 1) * G] = local.T
    for d in range(1, col_count):
        origin = col_at(d)
        remote(
            parts_out, parts_in.at[origin], part_send.at[d], part_recv.at[origin], row, origin
        ).wait_recv()
    sums = parts_in[0]
    for c in range(1, col_count):
        sums += parts_in[c]
    potential = weights[...] * jnp.tanh(sums)
    for t in range(tiles):
        high, low = split(turned[:, t * G : (t + 1) * G] * potential[t : t + 1, :])
        wh[:, t * G : (t + 1) * G] = high
        wl[:, t * G : (t + 1) * G] = low
    lanes = core.shape[0]
    stored = ks_slots * BS
    for d in range(1, col_count):
        origin = col_at(d)
        remote(
            square_out, square_in.at[origin], square_send.at[d], square_recv.at[origin], row, origin
        ).wait_recv()
    squares = square_in[0]
    for c in range(1, col_count):
        squares += square_in[c]
    square_all = jnp.broadcast_to(squares[0:1, 0:1], (8, lanes))

    def contribute(owner, out, i):
        at = pl.ds(pl.multiple_of(owner * lanes, PAIR), lanes)
        chunk[...] = dot3(wh[...], wl[...], bh[:, at], bl[:, at])
        for h in range(lanes // PAIR):
            here = slice(h * PAIR, (h + 1) * PAIR)
            for s in range(ks_slots):
                line_at = rows + row_blocks + h * ks_slots + s
                code = by_row[owner, line_at : line_at + 1, :]
                block = jnp.zeros((BS, PAIR), jnp.float32)
                for k in range(width // BS):
                    block += jnp.where(code == float(k), chunk[k * BS : (k + 1) * BS, here], 0.0)
                out[i, s * BS : (s + 1) * BS, here] = block
        out[i, stored : stored + 8, :] = square_all

    def pair_copy(i):
        return remote(
            pair_out.at[i], pair_in.at[i], pair_send.at[i], pair_recv.at[i], partner, col
        )

    def line_copy(i):
        return remote(
            mid.at[i], line_in.at[i], line_send.at[i], line_recv.at[i], on_line(i + 1), col
        )

    def join(i):
        pair_copy(i).wait_recv()
        mid[i] = mid[i] + pair_in[i]

    @pl.loop(0, line)
    def _(i):
        owner = on_line(i + 1)
        contribute(owner + 1 - 2 * side, pair_out, i)
        pair_copy(i).start()
        contribute(owner, mid, i)

        @pl.when(i >= 1)
        def _():
            join(i - 1)
            line_copy(i - 1).start()

    join(line - 1)
    result = mid[line - 1]
    for i in range(line - 1):
        line_copy(i).wait_recv()
        result += line_in[i]
    kohn[...] = core[...] + result[0:stored, :].T
    mean_square = result[stored : stored + 1, 0:1] / entry_count
    purified[...] = kept[...] / jnp.sqrt(mean_square + 1e-06)

    for copy in own_sends + passed + part_sends:
        copy.wait_send()
    for i in range(line):
        pair_copy(i).wait_send()
    for i in range(line - 1):
        line_copy(i).wait_send()


def plain(
    density_values, density_cols, ks_cols, core_hamiltonian, tile_blocks, grid_weights, basis_values
):
    highest = lax.Precision.HIGHEST
    row_blocks, own_slots = density_cols.shape
    ks_slots = ks_cols.shape[1]
    panel, panel_cols, panel_ks = (
        lax.all_gather(density_values, "row", axis=0, tiled=True),
        lax.all_gather(density_cols, "row", axis=0, tiled=True),
        lax.all_gather(ks_cols, "row", axis=0, tiled=True),
    )
    all_blocks = panel_cols.shape[0]
    panel_blocks = panel.reshape(all_blocks, BS, own_slots, BS)
    empty = jnp.zeros((row_blocks, BS, own_slots, BS), jnp.float32)
    values = lax.all_gather(density_values, "col", axis=1, tiled=True)
    columns = lax.all_gather(density_cols, "col", axis=1, tiled=True)
    width = columns.shape[1]
    left_blocks = values.reshape(row_blocks, BS, width, BS)
    neighbours = panel_blocks[columns]
    their_cols = panel_cols[columns]
    matches = (their_cols[:, :, :, None] == density_cols[:, None, None, :]).astype(jnp.float32)
    combined = jnp.einsum("ipqr,ipaqh->iprah", matches, neighbours, precision=highest)
    product = empty + jnp.einsum("ifpa,iprah->ifrh", left_blocks, combined, precision=highest)
    kept = product.reshape(row_blocks * BS, own_slots * BS)
    total_square = lax.psum(jnp.sum(kept * kept), ("row", "col"))
    entry_count = all_blocks * BS * own_slots * lax.axis_size("col") * BS
    purified = kept / jnp.sqrt(total_square / entry_count + 1e-06)
    tile_count = tile_blocks.shape[0]
    basis = basis_values.reshape(tile_count, G, TB, BS)
    tile_rows = panel_blocks[tile_blocks]
    tile_cols = panel_cols[tile_blocks]
    halves = jnp.einsum("tgif,tifqh->tgiqh", basis, tile_rows, precision=highest)
    matches = (tile_cols[:, :, :, None] == tile_blocks[:, None, None, :]).astype(jnp.float32)
    combined = jnp.einsum("tiqj,tgiqh->tgjh", matches, halves, precision=highest)
    partial_density = jnp.sum(combined * basis, axis=(2, 3))
    grid_density = lax.psum(partial_density, "col")
    potential = grid_weights * jnp.tanh(grid_density)
    weighted = basis * potential[:, :, None, None]
    ks_here = panel_ks[tile_blocks]
    ks_matches = (ks_here[:, :, :, None] == tile_blocks[:, None, None, :]).astype(jnp.float32)
    selected = jnp.einsum("tisj,tgjh->tgish", ks_matches, basis, precision=highest)
    pairs = jnp.einsum("tgif,tgish->tifsh", weighted, selected, precision=highest)
    ks_panel = jnp.zeros((all_blocks, BS, ks_slots, BS), jnp.float32)
    ks_panel = ks_panel.at[tile_blocks.reshape(-1)].add(
        pairs.reshape(tile_count * TB, BS, ks_slots, BS)
    )
    own_rows = lax.psum_scatter(
        ks_panel.reshape(all_blocks * BS, ks_slots * BS), "row", scatter_dimension=0, tiled=True
    )
    kohn_sham = core_hamiltonian + own_rows
    return (kohn_sham, purified)


def dense(
    density_values, density_cols, ks_cols, core_hamiltonian, tile_blocks, grid_weights, basis_values
):
    row_blocks, own_slots = density_cols.shape
    ks_slots = ks_cols.shape[1]
    row_count, col_count = lax.axis_size("row"), lax.axis_size("col")
    all_blocks = row_blocks * row_count
    col_blocks = all_blocks // col_count
    width = col_blocks * BS
    order = all_blocks * BS
    tiles = tile_blocks.shape[0]
    points = tiles * G
    rows = row_blocks * BS
    line = row_count // 2
    stored = ks_slots * BS
    f32, bf16 = jnp.float32, jnp.bfloat16
    vmem, smem = pl.BlockSpec(memory_space=pltpu.VMEM), pl.BlockSpec(memory_space=pltpu.SMEM)

    used = rows + row_blocks + ks_slots * (rows // PAIR)
    packed_rows = used + -used % 16

    blocks = jnp.arange(all_blocks, dtype=jnp.int32)
    index = jnp.arange(TB, dtype=jnp.int32)
    same = tile_blocks[:, :, None] == blocks[None, None, :]
    places = jnp.min(jnp.where(same, index[None, :, None], TB), axis=1).astype(jnp.int32)

    dma = pltpu.SemaphoreType.DMA
    kernel = functools.partial(
        mega_kernel,
        row_blocks=row_blocks,
        ks_slots=ks_slots,
        entry_count=float(order * own_slots * col_count * BS),
    )
    return tuple(
        pl.pallas_call(
            kernel,
            out_shape=[
                jax.ShapeDtypeStruct((rows, stored), f32),
                jax.ShapeDtypeStruct((rows, PAIR), f32),
            ],
            in_specs=[smem] * 3 + [pl.BlockSpec(memory_space=pl.ANY)] + [vmem] * 3,
            out_specs=[vmem, vmem],
            scratch_shapes=[
                pltpu.VMEM(basis_values.shape, f32),
                pltpu.VMEM((packed_rows, PAIR), f32),
                pltpu.VMEM((points, width), f32),
                pltpu.VMEM((8, PAIR), f32),
                pltpu.VMEM((col_count, 8, PAIR), f32),
                pltpu.VMEM((points, order), bf16),
                pltpu.VMEM((points, order), bf16),
                pltpu.VMEM((2, TB // 2 + 1, G, PAIR), f32),
                pltpu.VMEM((row_count, packed_rows, PAIR), f32),
                pltpu.VMEM((col_count, packed_rows, PAIR), f32),
                pltpu.VMEM((order, width), bf16),
                pltpu.VMEM((order, width), bf16),
                pltpu.VMEM((rows, order), bf16),
                pltpu.VMEM((rows, order), bf16),
                pltpu.VMEM((rows, width), f32),
                pltpu.VMEM((rows, PAIR), f32),
                pltpu.VMEM((tiles, PAIR), f32),
                pltpu.VMEM((col_count, tiles, PAIR), f32),
                pltpu.VMEM((width, points), f32),
                pltpu.VMEM((width, points), bf16),
                pltpu.VMEM((width, points), bf16),
                pltpu.VMEM((width, rows), f32),
                pltpu.VMEM((line, stored + 8, rows), f32),
                pltpu.VMEM((line, stored + 8, rows), f32),
                pltpu.VMEM((line, stored + 8, rows), f32),
                pltpu.VMEM((line, stored + 8, rows), f32),
                dma((line,)),
                dma((row_count,)),
                dma((line,)),
                dma((col_count,)),
                dma((col_count,)),
                dma((col_count,)),
                dma((col_count,)),
                dma((line,)),
                dma((line,)),
                dma((line,)),
                dma((line,)),
                dma((col_count,)),
                dma((col_count,)),
                dma,
            ],
            compiler_params=pltpu.CompilerParams(
                vmem_limit_bytes=VMEM_BUDGET, collective_id=0, has_side_effects=True
            ),
            cost_estimate=pl.CostEstimate(
                flops=12 * points * order * width,
                bytes_accessed=4 * points * TB * BS,
                transcendentals=points,
            ),
            name="kohn_sham_build",
        )(
            places, density_cols, ks_cols, basis_values, density_values, grid_weights, core_hamiltonian
        )
    )


def on_device(*args):
    density_cols, tile_blocks = args[1], args[4]
    all_blocks = density_cols.shape[0] * lax.axis_size("row")
    order = all_blocks * BS
    width = order // lax.axis_size("col")
    points = tile_blocks.shape[0] * G
    held = 4 * points * order + 4 * order * width + 4 * points * TB * BS
    fits = held + 24 * points * width < VMEM_BUDGET
    regular = density_cols.shape[1] * BS == PAIR and density_cols.shape[0] % 2 == 0
    regular = regular and lax.axis_size("row") % 2 == 0
    if fits and regular and width % PAIR == 0 and tile_blocks.shape[0] % 8 == 0:
        return dense(*args)
    return plain(*args)


def solution(mesh):
    in_specs = (
        P("row", "col"),
        P("row", "col"),
        P("row", "col"),
        P("row", "col"),
        P("row", None),
        P("row", None),
        P("row", None, None),
    )
    out_specs = (P("row", "col"), P("row", "col"))
    return jax.shard_map(
        on_device, mesh=mesh, in_specs=in_specs, out_specs=out_specs, check_vma=False
    )
```

```python
import functools
import jax
import jax.numpy as jnp
from jax import lax
from jax.experimental import pallas as pl
from jax.experimental.pallas import tpu as pltpu
from jax.sharding import PartitionSpec as P

BS = 64
TB = 16
G = 128
PAIR = 2 * BS
VMEM_BUDGET = 52 * 1024 * 1024


def split(x):
    high = x.astype(jnp.bfloat16)
    return high, (x - high.astype(jnp.float32)).astype(jnp.bfloat16)


def dot(a, b):
    return jnp.dot(a, b, preferred_element_type=jnp.float32)


def dot3(ah, al, bh, bl):
    return dot(ah, bh) + (dot(ah, bl) + dot(al, bh))


def lane_half():
    return (lax.broadcasted_iota(jnp.int32, (1, PAIR), 1) >= BS).astype(jnp.float32)


def widen(values, codes, out_h, out_l, row, first_lane, pairs):
    half = lane_half()
    swapped = pltpu.roll(values, BS, 1)
    swapped_codes = pltpu.roll(jnp.broadcast_to(codes, (8, PAIR)), BS, 1)[0:1]
    for p in range(pairs):
        block = 2.0 * p + half
        dense = jnp.where(codes == block, values, 0.0) + jnp.where(
            swapped_codes == block, swapped, 0.0
        )
        high, low = split(dense)
        lanes = pl.ds(first_lane + p * PAIR, PAIR)
        out_h[pl.ds(row, BS), lanes] = high
        out_l[pl.ds(row, BS), lanes] = low


MESH = pl.DeviceIdType.MESH


def mega_kernel(
    places, density_cols, ks_cols, basis_hbm, values, weights, core,
    kohn, purified,
    basis, packed, acc, square_out, square_in, bh, bl, sources, by_row, by_col, dh, dl, oh, ol, product, kept, parts_out, parts_in, turned, wh, wl,
    chunk, pair_out, pair_in, mid, line_in,
    row_send, row_recv, pass_send, col_send, col_recv, part_send, part_recv,
    pair_send, pair_recv, line_send, line_recv, square_send, square_recv, basis_sem,
    *, row_blocks, ks_slots, entry_count,
):
    row_count, col_count = by_row.shape[0], by_col.shape[0]
    row, col = lax.axis_index("row"), lax.axis_index("col")
    side, place = row % 2, row // 2
    line = row_count // 2
    partner = 2 * place + 1 - side
    rows = row_blocks * BS
    tiles = basis.shape[0]
    points = tiles * G
    width = dh.shape[1]
    pairs = width // PAIR
    half = lane_half()

    def on_line(d):
        return 2 * lax.rem(place + d, line) + side

    def col_at(d):
        return lax.rem(col + d, col_count)

    def remote(src, dst, send, recv, to_row, to_col):
        return pltpu.make_async_remote_copy(
            src_ref=src, dst_ref=dst, send_sem=send, recv_sem=recv,
            device_id=(to_row, to_col), device_id_type=MESH,
        )

    load_basis = pltpu.make_async_copy(basis_hbm, basis, basis_sem)
    load_basis.start()
    barrier = pltpu.get_barrier_semaphore()
    pl.semaphore_signal(barrier, inc=1, device_id=(partner, col), device_id_type=MESH)
    for d in range(1, line):
        pl.semaphore_signal(barrier, inc=1, device_id=(on_line(d), col), device_id_type=MESH)
    for d in range(1, col_count):
        pl.semaphore_signal(barrier, inc=1, device_id=(row, col_at(d)), device_id_type=MESH)
    base = col * (width // BS)

    def code_line(left, right):
        both = jnp.where(half == 0.0, left - base, right - base)
        return both.astype(jnp.float32)

    packed[0:rows, :] = values[...]
    for l in range(row_blocks):
        packed[rows + l : rows + l + 1, :] = code_line(density_cols[l, 0], density_cols[l, 1])
    used = rows + row_blocks
    for h in range(row_blocks // 2):
        for slot in range(ks_slots):
            packed[used : used + 1, :] = code_line(ks_cols[2 * h, slot], ks_cols[2 * h + 1, slot])
            used += 1
    if used < packed.shape[0]:
        packed[used:, :] = jnp.zeros((packed.shape[0] - used, PAIR), jnp.float32)
    pl.semaphore_wait(barrier, line + col_count - 1)

    own_sends = []
    for d in range(1, line):
        own_sends.append(
            remote(packed, by_row.at[row], row_send.at[d], row_recv.at[row], on_line(d), col)
        )
    own_sends.append(remote(packed, by_row.at[row], row_send.at[0], row_recv.at[row], partner, col))
    for d in range(1, col_count):
        own_sends.append(
            remote(packed, by_col.at[col], col_send.at[d], col_recv.at[col], row, col_at(d))
        )
    for copy in own_sends:
        copy.start()
    by_row[row] = packed[...]
    by_col[col] = packed[...]

    source_pairs = basis.shape[2] // PAIR
    sources[0, source_pairs] = jnp.zeros((G, PAIR), jnp.float32)
    sources[1, source_pairs] = jnp.zeros((G, PAIR), jnp.float32)

    def expand(t):
        for p in range(source_pairs):
            x = basis[t, :, p * PAIR : (p + 1) * PAIR]
            sources[0, p] = x
            sources[1, p] = pltpu.roll(x, BS, 1)
        at = pl.ds(pl.multiple_of(t * G, G), G)
        for d in range(bh.shape[1] // PAIR):
            left = places[t, 2 * d]
            right = places[t, 2 * d + 1]
            dense = jnp.where(
                half == 0.0,
                sources[left % 2, left // 2],
                sources[1 - right % 2, right // 2],
            )
            high, low = split(dense)
            bh[at, d * PAIR : (d + 1) * PAIR] = high
            bl[at, d * PAIR : (d + 1) * PAIR] = low

    acc[...] = jnp.zeros(acc.shape, jnp.float32)
    load_basis.wait()
    first = tiles // 2 if line > 1 else tiles
    pl.loop(0, first)(expand)

    def widen_row(r):
        for l in range(row_blocks):
            at = pl.multiple_of((r * row_blocks + l) * BS, BS)
            widen(
                by_row[r, l * BS : (l + 1) * BS, :],
                by_row[r, rows + l : rows + l + 1, :],
                dh, dl, at, 0, pairs,
            )

    step = 4 * G

    def absorb(r):
        widen_row(r)
        deep = pl.ds(pl.multiple_of(r * rows, PAIR), rows)

        @pl.loop(0, points // step)
        def _(s):
            at = pl.ds(pl.multiple_of(s * step, step), step)
            acc[at, :] += dot3(bh[at, deep], bl[at, deep], dh[deep, :], dl[deep, :])

    passed = []
    for d in range(1, line):
        origin = 2 * lax.rem(place + line - d, line) + side
        remote(
            packed, by_row.at[origin], row_send.at[d], row_recv.at[origin], partner, col
        ).wait_recv()
        copy = remote(
            by_row.at[origin], by_row.at[origin], pass_send.at[d], row_recv.at[origin], partner, col
        )
        copy.start()
        passed.append(copy)
        if d == 1:
            pl.loop(first, tiles)(expand)
        else:
            absorb(2 * lax.rem(place + line - d + 2, line) + side)

    @pl.loop(max(line - 2, 0), line)
    def _(d):
        absorb(2 * lax.rem(place + line - d, line) + side)

    @pl.loop(0, line)
    def _(d):
        origin = 2 * lax.rem(place + line - d, line) + 1 - side
        remote(
            packed, by_row.at[origin], row_send.at[0], row_recv.at[origin], partner, col
        ).wait_recv()
        absorb(origin)

    mine = pl.ds(pl.multiple_of(col * width, PAIR), width)

    @pl.loop(0, tiles)
    def _(t):
        at = pl.ds(pl.multiple_of(t * G, G), G)
        local = bh[at, mine].astype(jnp.float32) + bl[at, mine].astype(jnp.float32)
        sums = jnp.sum(acc[at, :] * local, axis=1, keepdims=True)
        parts_out[pl.ds(t, 1), :] = jnp.broadcast_to(sums, (G, G)).T[0:1, :]

    part_sends = []
    for d in range(1, col_count):
        copy = remote(
            parts_out, parts_in.at[col], part_send.at[d], part_recv.at[col], row, col_at(d)
        )
        copy.start()
        part_sends.append(copy)
    parts_in[col] = parts_out[...]

    for d in range(1, col_count):
        origin = col_at(d)
        remote(
            packed, by_col.at[origin], col_send.at[d], col_recv.at[origin], row, origin
        ).wait_recv()
    for c in range(col_count):
        for l in range(row_blocks):
            widen(
                by_col[c, l * BS : (l + 1) * BS, :],
                by_col[c, rows + l : rows + l + 1, :],
                oh, ol, l * BS, c * width, pairs,
            )
    product[...] = dot3(oh[...], ol[...], dh[...], dl[...])
    total = jnp.zeros((BS, PAIR), jnp.float32)
    for l in range(row_blocks):
        codes_here = packed[rows + l : rows + l + 1, :]
        block = jnp.zeros((BS, PAIR), jnp.float32)
        for p in range(pairs):
            piece = product[l * BS : (l + 1) * BS, p * PAIR : (p + 1) * PAIR]
            block += jnp.where(codes_here == 2.0 * p + half, piece, 0.0)
            block += jnp.where(
                codes_here == 2.0 * p + 1.0 - half, pltpu.roll(piece, BS, 1), 0.0
            )
        kept[l * BS : (l + 1) * BS, :] = block
        total += block * block
    square = jnp.sum(jnp.sum(total, axis=1, keepdims=True), axis=0, keepdims=True)
    square_out[...] = jnp.broadcast_to(square, (8, PAIR))
    for d in range(1, col_count):
        copy = remote(
            square_out, square_in.at[col], square_send.at[d], square_recv.at[col], row, col_at(d)
        )
        copy.start()
        part_sends.append(copy)
    square_in[col] = square_out[...]
    for t in range(tiles):
        at = pl.ds(t * G, G)
        local = bh[at, mine].astype(jnp.float32) + bl[at, mine].astype(jnp.float32)
        turned[:, t * G : (t + 1) * G] = local.T
    for d in range(1, col_count):
        origin = col_at(d)
        remote(
            parts_out, parts_in.at[origin], part_send.at[d], part_recv.at[origin], row, origin
        ).wait_recv()
    sums = parts_in[0]
    for c in range(1, col_count):
        sums += parts_in[c]
    potential = weights[...] * jnp.tanh(sums)
    for t in range(tiles):
        high, low = split(turned[:, t * G : (t + 1) * G] * potential[t : t + 1, :])
        wh[:, t * G : (t + 1) * G] = high
        wl[:, t * G : (t + 1) * G] = low
    lanes = core.shape[0]
    stored = ks_slots * BS
    for d in range(1, col_count):
        origin = col_at(d)
        remote(
            square_out, square_in.at[origin], square_send.at[d], square_recv.at[origin], row, origin
        ).wait_recv()
    squares = square_in[0]
    for c in range(1, col_count):
        squares += square_in[c]
    square_all = jnp.broadcast_to(squares[0:1, 0:1], (8, lanes))

    def contribute(owner, out, i):
        at = pl.ds(pl.multiple_of(owner * lanes, PAIR), lanes)
        chunk[...] = dot3(wh[...], wl[...], bh[:, at], bl[:, at])
        for h in range(lanes // PAIR):
            here = slice(h * PAIR, (h + 1) * PAIR)
            for s in range(ks_slots):
                line_at = rows + row_blocks + h * ks_slots + s
                code = by_row[owner, line_at : line_at + 1, :]
                block = jnp.zeros((BS, PAIR), jnp.float32)
                for k in range(width // BS):
                    block += jnp.where(code == float(k), chunk[k * BS : (k + 1) * BS, here], 0.0)
                out[i, s * BS : (s + 1) * BS, here] = block
        out[i, stored : stored + 8, :] = square_all

    def pair_copy(i):
        return remote(
            pair_out.at[i], pair_in.at[i], pair_send.at[i], pair_recv.at[i], partner, col
        )

    def line_copy(i):
        return remote(
            mid.at[i], line_in.at[i], line_send.at[i], line_recv.at[i], on_line(i + 1), col
        )

    def join(i):
        pair_copy(i).wait_recv()
        mid[i] = mid[i] + pair_in[i]

    @pl.loop(0, line)
    def _(i):
        owner = on_line(i + 1)
        contribute(owner + 1 - 2 * side, pair_out, i)
        pair_copy(i).start()
        contribute(owner, mid, i)

        @pl.when(i >= 1)
        def _():
            join(i - 1)
            line_copy(i - 1).start()

    join(line - 1)
    result = mid[line - 1]
    for i in range(line - 1):
        line_copy(i).wait_recv()
        result += line_in[i]
    kohn[...] = core[...] + result[0:stored, :].T
    mean_square = result[stored : stored + 1, 0:1] / entry_count
    purified[...] = kept[...] / jnp.sqrt(mean_square + 1e-06)

    for copy in own_sends + passed + part_sends:
        copy.wait_send()
    for i in range(line):
        pair_copy(i).wait_send()
    for i in range(line - 1):
        line_copy(i).wait_send()


def plain(
    density_values, density_cols, ks_cols, core_hamiltonian, tile_blocks, grid_weights, basis_values
):
    highest = lax.Precision.HIGHEST
    row_blocks, own_slots = density_cols.shape
    ks_slots = ks_cols.shape[1]
    panel, panel_cols, panel_ks = (
        lax.all_gather(density_values, "row", axis=0, tiled=True),
        lax.all_gather(density_cols, "row", axis=0, tiled=True),
        lax.all_gather(ks_cols, "row", axis=0, tiled=True),
    )
    all_blocks = panel_cols.shape[0]
    panel_blocks = panel.reshape(all_blocks, BS, own_slots, BS)
    empty = jnp.zeros((row_blocks, BS, own_slots, BS), jnp.float32)
    values = lax.all_gather(density_values, "col", axis=1, tiled=True)
    columns = lax.all_gather(density_cols, "col", axis=1, tiled=True)
    width = columns.shape[1]
    left_blocks = values.reshape(row_blocks, BS, width, BS)
    neighbours = panel_blocks[columns]
    their_cols = panel_cols[columns]
    matches = (their_cols[:, :, :, None] == density_cols[:, None, None, :]).astype(jnp.float32)
    combined = jnp.einsum("ipqr,ipaqh->iprah", matches, neighbours, precision=highest)
    product = empty + jnp.einsum("ifpa,iprah->ifrh", left_blocks, combined, precision=highest)
    kept = product.reshape(row_blocks * BS, own_slots * BS)
    total_square = lax.psum(jnp.sum(kept * kept), ("row", "col"))
    entry_count = all_blocks * BS * own_slots * lax.axis_size("col") * BS
    purified = kept / jnp.sqrt(total_square / entry_count + 1e-06)
    tile_count = tile_blocks.shape[0]
    basis = basis_values.reshape(tile_count, G, TB, BS)
    tile_rows = panel_blocks[tile_blocks]
    tile_cols = panel_cols[tile_blocks]
    halves = jnp.einsum("tgif,tifqh->tgiqh", basis, tile_rows, precision=highest)
    matches = (tile_cols[:, :, :, None] == tile_blocks[:, None, None, :]).astype(jnp.float32)
    combined = jnp.einsum("tiqj,tgiqh->tgjh", matches, halves, precision=highest)
    partial_density = jnp.sum(combined * basis, axis=(2, 3))
    grid_density = lax.psum(partial_density, "col")
    potential = grid_weights * jnp.tanh(grid_density)
    weighted = basis * potential[:, :, None, None]
    ks_here = panel_ks[tile_blocks]
    ks_matches = (ks_here[:, :, :, None] == tile_blocks[:, None, None, :]).astype(jnp.float32)
    selected = jnp.einsum("tisj,tgjh->tgish", ks_matches, basis, precision=highest)
    pairs = jnp.einsum("tgif,tgish->tifsh", weighted, selected, precision=highest)
    ks_panel = jnp.zeros((all_blocks, BS, ks_slots, BS), jnp.float32)
    ks_panel = ks_panel.at[tile_blocks.reshape(-1)].add(
        pairs.reshape(tile_count * TB, BS, ks_slots, BS)
    )
    own_rows = lax.psum_scatter(
        ks_panel.reshape(all_blocks * BS, ks_slots * BS), "row", scatter_dimension=0, tiled=True
    )
    kohn_sham = core_hamiltonian + own_rows
    return (kohn_sham, purified)


def dense(
    density_values, density_cols, ks_cols, core_hamiltonian, tile_blocks, grid_weights, basis_values
):
    row_blocks, own_slots = density_cols.shape
    ks_slots = ks_cols.shape[1]
    row_count, col_count = lax.axis_size("row"), lax.axis_size("col")
    all_blocks = row_blocks * row_count
    col_blocks = all_blocks // col_count
    width = col_blocks * BS
    order = all_blocks * BS
    tiles = tile_blocks.shape[0]
    points = tiles * G
    rows = row_blocks * BS
    line = row_count // 2
    stored = ks_slots * BS
    f32, bf16 = jnp.float32, jnp.bfloat16
    vmem, smem = pl.BlockSpec(memory_space=pltpu.VMEM), pl.BlockSpec(memory_space=pltpu.SMEM)

    used = rows + row_blocks + ks_slots * (rows // PAIR)
    packed_rows = used + -used % 16

    blocks = jnp.arange(all_blocks, dtype=jnp.int32)
    index = jnp.arange(TB, dtype=jnp.int32)
    same = tile_blocks[:, :, None] == blocks[None, None, :]
    places = jnp.min(jnp.where(same, index[None, :, None], TB), axis=1).astype(jnp.int32)

    dma = pltpu.SemaphoreType.DMA
    kernel = functools.partial(
        mega_kernel,
        row_blocks=row_blocks,
        ks_slots=ks_slots,
        entry_count=float(order * own_slots * col_count * BS),
    )
    return tuple(
        pl.pallas_call(
            kernel,
            out_shape=[
                jax.ShapeDtypeStruct((rows, stored), f32),
                jax.ShapeDtypeStruct((rows, PAIR), f32),
            ],
            in_specs=[smem] * 3 + [pl.BlockSpec(memory_space=pl.ANY)] + [vmem] * 3,
            out_specs=[vmem, vmem],
            scratch_shapes=[
                pltpu.VMEM(basis_values.shape, f32),
                pltpu.VMEM((packed_rows, PAIR), f32),
                pltpu.VMEM((points, width), f32),
                pltpu.VMEM((8, PAIR), f32),
                pltpu.VMEM((col_count, 8, PAIR), f32),
                pltpu.VMEM((points, order), bf16),
                pltpu.VMEM((points, order), bf16),
                pltpu.VMEM((2, TB // 2 + 1, G, PAIR), f32),
                pltpu.VMEM((row_count, packed_rows, PAIR), f32),
                pltpu.VMEM((col_count, packed_rows, PAIR), f32),
                pltpu.VMEM((order, width), bf16),
                pltpu.VMEM((order, width), bf16),
                pltpu.VMEM((rows, order), bf16),
                pltpu.VMEM((rows, order), bf16),
                pltpu.VMEM((rows, width), f32),
                pltpu.VMEM((rows, PAIR), f32),
                pltpu.VMEM((tiles, PAIR), f32),
                pltpu.VMEM((col_count, tiles, PAIR), f32),
                pltpu.VMEM((width, points), f32),
                pltpu.VMEM((width, points), bf16),
                pltpu.VMEM((width, points), bf16),
                pltpu.VMEM((width, rows), f32),
                pltpu.VMEM((line, stored + 8, rows), f32),
                pltpu.VMEM((line, stored + 8, rows), f32),
                pltpu.VMEM((line, stored + 8, rows), f32),
                pltpu.VMEM((line, stored + 8, rows), f32),
                dma((line,)),
                dma((row_count,)),
                dma((line,)),
                dma((col_count,)),
                dma((col_count,)),
                dma((col_count,)),
                dma((col_count,)),
                dma((line,)),
                dma((line,)),
                dma((line,)),
                dma((line,)),
                dma((col_count,)),
                dma((col_count,)),
                dma,
            ],
            compiler_params=pltpu.CompilerParams(
                vmem_limit_bytes=VMEM_BUDGET, collective_id=0, has_side_effects=True
            ),
            cost_estimate=pl.CostEstimate(
                flops=12 * points * order * width,
                bytes_accessed=4 * points * TB * BS,
                transcendentals=points,
            ),
            name="kohn_sham_build",
        )(
            places, density_cols, ks_cols, basis_values, density_values, grid_weights, core_hamiltonian
        )
    )


def on_device(*args):
    density_cols, tile_blocks = args[1], args[4]
    all_blocks = density_cols.shape[0] * lax.axis_size("row")
    order = all_blocks * BS
    width = order // lax.axis_size("col")
    points = tile_blocks.shape[0] * G
    held = 4 * points * order + 4 * order * width + 4 * points * TB * BS
    fits = held + 24 * points * width < VMEM_BUDGET
    regular = density_cols.shape[1] * BS == PAIR and density_cols.shape[0] % 2 == 0
    regular = regular and lax.axis_size("row") % 2 == 0
    if fits and regular and width % PAIR == 0 and tile_blocks.shape[0] % 8 == 0:
        return dense(*args)
    return plain(*args)


def solution(mesh):
    in_specs = (
        P("row", "col"),
        P("row", "col"),
        P("row", "col"),
        P("row", "col"),
        P("row", None),
        P("row", None),
        P("row", None, None),
    )
    out_specs = (P("row", "col"), P("row", "col"))
    return jax.shard_map(
        on_device, mesh=mesh, in_specs=in_specs, out_specs=out_specs, check_vma=False
    )
```
